32 devices in a mesh: rep: 2 (over y), exp: 16 (over z, x, core).
Axes of the slice: x: 2, y: 2, z: 4, core: 2. Of those that a mesh axis runs over, the one named last changes fastest.
Arguments:
- tokens: bfloat16 [4096, 1024], P(('rep', 'exp')), may hold values from -6 to 6
- cotangent: bfloat16 [4096, 1024], P(('rep', 'exp')), may hold values from -6 to 6
- expert_ids: int32 [4096, 2], P(('rep', 'exp')), may hold values from 0 to 15, all different within a row; in each aligned block of 128 rows (0 to 127, 128 to 255, ...) at most 32 rows name the same one
- combine_weight: float32 [4096, 2], P(('rep', 'exp')), may hold values from 0.2 to 1
- gate_weight: bfloat16 [16, 1024, 768], P('exp', 'rep'), may hold values from -0.1875 to 0.1875
- up_weight: bfloat16 [16, 1024, 768], P('exp', 'rep'), may hold values from -0.1875 to 0.1875
- down_weight: bfloat16 [16, 768, 1024], P('exp', None, 'rep'), may hold values from -0.21875 to 0.21875
Outputs:
- mixed: bfloat16 [4096, 1024], P(('rep', 'exp'))
- token_grad: bfloat16 [4096, 1024], P(('rep', 'exp'))
- gate_grad: bfloat16 [16, 1024, 768], P('exp', 'rep')
- up_grad: bfloat16 [16, 1024, 768], P('exp', 'rep')
- down_grad: bfloat16 [16, 768, 1024], P('exp', None, 'rep')
The draws below stay inside these ranges and needn't reach their ends.
Inputs may be any that keep to these rules, and one draw needn't show every extreme that they name: `expert_ids`: each token names 2 different experts. Among the 128 tokens of one aligned block of rows, no expert is named more than 32 times, and in some block an expert is named exactly 32 times.
All inputs are finite; a program needn't handle non-finite values.
Results may differ from the reference program's by a relative error of at most 0.014.
Values may be sent and summed in bfloat16 or wider, within the bound.
A program may use at most 64 MiB of HBM per device.

```python
import math
import jax
import jax.numpy as jnp
import numpy as np
from jax import lax

D = 1024
FF = 768
TOP = 2
TOK_DEV = 128
EXPERTS = 16
CAP = 32
TOKENS = 4096
N_REP = 2
N_EXP = 16


def levels(stream_key, dims, pieces, smallest, high):
    def one(dim, shards_of):
        heights = jax.random.uniform(jax.random.fold_in(jax.random.fold_in(stream_key, 6), dim), (shards_of,), jnp.float32, smallest / len(pieces), high / len(pieces))
        return jnp.repeat(jnp.exp(heights), dims[dim] // shards_of).reshape((-1,) + (1,) * (len(dims) - dim - 1))

    loudness = one(*pieces[0])
    for cut in pieces[1:]:
        loudness = loudness * one(*cut)
    return loudness


def routed_block(own_key, own, number, rows, count, top, reach, slope):
    ranking = jax.random.permutation(own_key, count)
    packed, common = shares(count, rows * top, reach, slope, True), shares(count, rows * top, reach, slope, False)
    places = jnp.arange(count)

    def named(sizes, offset_by):
        used = int((sizes > 0).sum())
        fixed = max(1, used // 4)
        moved = fixed + (places - fixed + offset_by * (used - fixed)) % max(1, count - fixed)
        return jnp.zeros((count,), jnp.int32).at[ranking[jnp.where(places < fixed, places, moved)]].set(jnp.asarray(sizes, jnp.int32))

    sizes = jnp.where(number % 4 == 0, named(packed, number // 4), named(common, number - number // 4 - 1))
    mixed = jax.random.permutation(jax.random.fold_in(own, 3), count)
    giver, receiver = mixed[0:count // 2 * 2:2], mixed[1:count // 2 * 2:2]
    slack = jnp.minimum(sizes[giver] - 1, reach - sizes[receiver]) // 2
    slack = jnp.where((giver == ranking[0]) | (receiver == ranking[0]) | (sizes[receiver] == 0), 0, jnp.maximum(slack, 0))
    moved = jax.random.randint(jax.random.fold_in(own, 4), (count // 2,), 0, 1 << 20) % (slack + 1)
    sizes = sizes.at[giver].add(-moved).at[receiver].add(moved)
    members = jnp.searchsorted(jnp.cumsum(sizes), jnp.arange(rows * top), side="right").astype(jnp.int32)
    listing = members.reshape(top, rows).T
    listing = listing[jax.random.permutation(jax.random.fold_in(own, 1), rows)]
    offset_by = jax.random.randint(jax.random.fold_in(own, 2), (rows, 1), 0, top)
    return jnp.take_along_axis(listing, (jnp.arange(top)[None, :] + offset_by) % top, axis=1)


def shares(number_of, total, reach, slope, full):
    loads = [(1 << 20) // math.isqrt(rank ** slope) + 1 for rank in range(1, number_of + 1)]
    largest = reach if full else min(reach, max(-(-total // number_of), total * loads[0] // sum(loads)))
    least = 1 if total - largest >= number_of - 1 else 0
    counts, surplus = [largest] + [least] * (number_of - 1), total - largest - least * (number_of - 1)
    while surplus > 0:
        free = [i for i in range(1, number_of) if counts[i] < largest] or [i for i in range(1, number_of) if counts[i] < reach]
        pool, left = sum([loads[i] for i in free]), surplus
        for i in free:
            extra = min(reach - counts[i], max(1, left * loads[i] // pool), surplus)
            counts[i] = counts[i] + extra
            surplus = surplus - extra
    return np.array(counts)


def centred(key, extent, width, most, split=(), kind=jnp.bfloat16):
    values = jax.random.normal(key, extent, jnp.float32) * width
    if len(split) > 0:
        values = levels(key, extent, split, -0.22, 0.18) * values
    return jnp.clip(values, min=-most, max=most).astype(kind)


def setup_inputs(seed: int = 0) -> dict:
    keys = jax.random.split(jax.random.key(seed), 8)
    tokens = centred(keys[0], (TOKENS, D), 1.0, 6.0, ((0, 32),))
    cotangent = centred(keys[1], (TOKENS, D), 1.0, 6.0, ((0, 32),))
    expert_ids_keys = jax.random.split(jax.random.fold_in(keys[2], 1), TOKENS // TOK_DEV)
    expert_ids_turns = jax.random.permutation(jax.random.fold_in(keys[2], 3), TOKENS // TOK_DEV)
    expert_ids = jax.vmap(lambda own, number: routed_block(jax.random.fold_in(keys[2], 2), own, number, TOK_DEV, EXPERTS, TOP, CAP, 2))(expert_ids_keys, expert_ids_turns).reshape((TOKENS, TOP))
    combine_weight = jnp.clip(0.2 + 0.8 * jax.random.uniform(keys[3], (TOKENS, TOP), jnp.float32) ** levels(keys[3], (TOKENS, TOP), ((0, 32),), -0.2, 0.2), 0.2, 1.0)
    gate_weight = centred(keys[4], (EXPERTS, D, FF), D ** -0.5, 0.1875, ((0, 16), (1, 2)))
    up_weight = centred(keys[5], (EXPERTS, D, FF), D ** -0.5, 0.1875, ((0, 16), (1, 2)))
    down_weight = centred(keys[6], (EXPERTS, FF, D), FF ** -0.5, 0.21875, ((0, 16), (2, 2)))
    return dict(tokens=tokens, cotangent=cotangent, expert_ids=expert_ids, combine_weight=combine_weight, gate_weight=gate_weight, up_weight=up_weight, down_weight=down_weight)


def slot_index(block_ids):
    flat = block_ids.reshape(-1).astype(jnp.int32)
    onehot = (flat[:, None] == jnp.arange(EXPERTS, dtype=jnp.int32)[None, :]).astype(jnp.int32)
    before = jnp.cumsum(onehot, axis=0) - onehot
    return (flat * CAP + jnp.sum(before * onehot, axis=1)).astype(jnp.int32)


def reference(tokens, cotangent, expert_ids, combine_weight, gate_weight, up_weight, down_weight):
    devices_all = N_REP * N_EXP
    pair_count = TOK_DEV * TOP
    block_ids = expert_ids.reshape(devices_all, TOK_DEV, TOP)
    destination = jax.vmap(slot_index)(block_ids)
    device_rows = jnp.arange(devices_all, dtype=jnp.int32)[:, None]
    inverse = jnp.full((devices_all, EXPERTS * CAP), pair_count, jnp.int32)
    pair_numbers = jnp.broadcast_to(jnp.arange(pair_count, dtype=jnp.int32)[None, :], (devices_all, pair_count))
    inverse = inverse.at[device_rows, destination].set(pair_numbers)
    token_rows = tokens.reshape(devices_all, TOK_DEV, D)
    zero_row = jnp.zeros((devices_all, 1, D), tokens.dtype)
    x_pairs = jnp.concatenate([jnp.repeat(token_rows, TOP, axis=1), zero_row], axis=1)
    weighted = (combine_weight.reshape(devices_all, TOK_DEV, TOP, 1).astype(jnp.float32)
                * cotangent.reshape(devices_all, TOK_DEV, 1, D).astype(jnp.float32)).astype(jnp.bfloat16)
    c_pairs = jnp.concatenate([weighted.reshape(devices_all, pair_count, D), zero_row.astype(jnp.bfloat16)], axis=1)
    weight_pairs = jnp.concatenate([combine_weight.reshape(devices_all, pair_count).astype(jnp.float32),
                                    jnp.zeros((devices_all, 1), jnp.float32)], axis=1)

    def per_expert(carry, expert):
        out_acc, grad_acc = carry
        index = lax.dynamic_slice_in_dim(inverse, (expert * CAP).astype(jnp.int32), CAP, 1)
        block_x = jnp.take_along_axis(x_pairs, index[:, :, None], axis=1).reshape(devices_all * CAP, D)
        block_c = jnp.take_along_axis(c_pairs, index[:, :, None], axis=1).reshape(devices_all * CAP, D)
        w_gate = gate_weight[expert]
        w_up = up_weight[expert]
        w_down = down_weight[expert]
        gate_value = jnp.dot(block_x, w_gate, preferred_element_type=jnp.float32)
        up_value = jnp.dot(block_x, w_up, preferred_element_type=jnp.float32)
        swish_value = jax.nn.silu(gate_value)
        hidden = (swish_value * up_value).astype(jnp.bfloat16)
        output = jnp.dot(hidden, w_down, preferred_element_type=jnp.float32).astype(jnp.bfloat16)
        grad_hidden = lax.dot_general(block_c, w_down, (((1,), (1,)), ((), ())), preferred_element_type=jnp.float32)
        sigma = jax.nn.sigmoid(gate_value)
        grad_gate = (grad_hidden * up_value * sigma * (1.0 + gate_value * (1.0 - sigma))).astype(jnp.bfloat16)
        grad_up = (grad_hidden * swish_value).astype(jnp.bfloat16)
        grad_rows = (lax.dot_general(grad_gate, w_gate, (((1,), (1,)), ((), ())), preferred_element_type=jnp.float32)
                     + lax.dot_general(grad_up, w_up, (((1,), (1,)), ((), ())), preferred_element_type=jnp.float32)).astype(jnp.bfloat16)
        rep_x = block_x.reshape(N_REP, N_EXP * CAP, D).astype(jnp.float32)
        rep_c = block_c.reshape(N_REP, N_EXP * CAP, D).astype(jnp.float32)
        rep_gate = grad_gate.reshape(N_REP, N_EXP * CAP, FF).astype(jnp.float32)
        rep_up = grad_up.reshape(N_REP, N_EXP * CAP, FF).astype(jnp.float32)
        rep_hidden = hidden.reshape(N_REP, N_EXP * CAP, FF).astype(jnp.float32)
        part_gate = jnp.einsum('rmd,rmf->rdf', rep_x, rep_gate).astype(jnp.bfloat16)
        part_up = jnp.einsum('rmd,rmf->rdf', rep_x, rep_up).astype(jnp.bfloat16)
        part_down = jnp.einsum('rmf,rmd->rfd', rep_hidden, rep_c).astype(jnp.bfloat16)
        total_gate = (jnp.sum(part_gate.astype(jnp.float32), axis=0) / N_REP).astype(jnp.bfloat16)
        total_up = (jnp.sum(part_up.astype(jnp.float32), axis=0) / N_REP).astype(jnp.bfloat16)
        total_down = (jnp.sum(part_down.astype(jnp.float32), axis=0) / N_REP).astype(jnp.bfloat16)
        target_token = (index // TOP).astype(jnp.int32)
        slot_weight = jnp.take_along_axis(weight_pairs, index, axis=1)
        out_acc = out_acc.at[device_rows, target_token].add(
            slot_weight[:, :, None] * output.reshape(devices_all, CAP, D).astype(jnp.float32))
        grad_acc = grad_acc.at[device_rows, target_token].add(
            grad_rows.reshape(devices_all, CAP, D).astype(jnp.float32))
        return (out_acc, grad_acc), (total_gate, total_up, total_down)

    start = (jnp.zeros((devices_all, TOK_DEV + 1, D), jnp.float32), jnp.zeros((devices_all, TOK_DEV + 1, D), jnp.float32))
    (out_acc, grad_acc), (gate_grad, up_grad, down_grad) = lax.scan(
        per_expert, start, jnp.arange(EXPERTS, dtype=jnp.int32))
    mixed = out_acc[:, :TOK_DEV].reshape(TOKENS, D).astype(jnp.bfloat16)
    token_grad = grad_acc[:, :TOK_DEV].reshape(TOKENS, D).astype(jnp.bfloat16)
    return (mixed, token_grad, gate_grad, up_grad, down_grad)
```

```python
import functools

import jax
import jax.numpy as jnp
from jax import lax
from jax.experimental import pallas as pl
from jax.experimental.pallas import tpu as pltpu
from jax.sharding import PartitionSpec as P

MESH = pl.DeviceIdType.MESH
F32, BF16 = jnp.float32, jnp.bfloat16
NN = (((1,), (0,)), ((), ()))
NT = (((1,), (1,)), ((), ()))
TN = (((0,), (0,)), ((), ()))


def mm(a, b, dims):
    return lax.dot_general(a, b, dims, preferred_element_type=F32)


def rows_2d(block):
    groups, capacity, features = block.shape
    if capacity % 16:
        return block.astype(F32).reshape(groups * capacity, features).astype(BF16)
    return block.reshape(groups * capacity, features)


def kernel(
    reps, groups, cap, width,
    tok, cot, ids, cw, wg, wu, wd,
    mixed, token_grad, gate_grad, up_grad, down_grad,
    send_x, send_c, send_o, send_d, recv_x, recv_c, recv_o, recv_d,
    full_g, full_u, full_d, hid, d_gate, d_up,
    part_g, part_u, part_d, red_g, red_u, red_d,
    pick, pick_hi, pick_lo,
    a_send, a_recv, w_send, w_recv, g_send, g_recv, local_sem,
):
    rep, exp = lax.axis_index("rep"), lax.axis_index("exp")
    tokens, features = tok.shape
    share, hidden = wg.shape
    chunks = hidden // width
    rows = groups * cap
    mine = pl.ds(pl.multiple_of(rep * share, share), share)

    def cols(c):
        if isinstance(c, int):
            return pl.ds(c * width, width)
        return pl.ds(pl.multiple_of(c * width, width), width)

    barrier = pltpu.get_barrier_semaphore()

    def greet(i, carry):
        pl.semaphore_signal(
            barrier, inc=1, device_id=(rep, lax.rem(exp + i, groups)), device_id_type=MESH
        )
        return carry

    lax.fori_loop(1, groups, greet, 0)
    for j in range(1, reps):
        pl.semaphore_signal(
            barrier, inc=1, device_id=(lax.rem(rep + j, reps), exp), device_id_type=MESH
        )

    own_copies = [
        pltpu.make_async_copy(wg, full_g.at[mine, :], local_sem.at[0]),
        pltpu.make_async_copy(wu, full_u.at[mine, :], local_sem.at[1]),
        pltpu.make_async_copy(wd, full_d.at[:, mine], local_sem.at[2]),
    ]
    for copy in own_copies:
        copy.start()

    lanes = 128
    expert = lax.broadcasted_iota(jnp.int32, (tokens, lanes), 1)
    id_val = ids[...]
    cw_val = cw[...]
    hot = [(id_val[:, k : k + 1] == expert).astype(F32) for k in range(2)]
    earlier = (
        lax.broadcasted_iota(jnp.int32, (tokens, tokens), 1)
        < lax.broadcasted_iota(jnp.int32, (tokens, tokens), 0)
    )
    before = mm(earlier.astype(F32).astype(BF16), (hot[0] + hot[1]).astype(BF16), NN)
    place = before + (expert * cap).astype(F32)
    dest = [jnp.sum(hot[k] * place, axis=1, keepdims=True) for k in range(2)]
    table = jnp.where(
        expert == 0, dest[0],
        jnp.where(expert == 1, dest[1],
                  jnp.where(expert == 2, cw_val[:, 0:1],
                            jnp.where(expert == 3, cw_val[:, 1:2], 0.0))),
    )
    flipped = jnp.transpose(table)
    down_rows = lax.broadcasted_iota(jnp.int32, (rows, tokens), 0).astype(F32)
    sel0 = (down_rows == flipped[0:1, :]).astype(F32)
    sel1 = (down_rows == flipped[1:2, :]).astype(F32)
    select = (sel0 + sel1).astype(BF16)
    row_weight = jnp.sum(
        sel0 * flipped[2:3, :] + sel1 * flipped[3:4, :], axis=1, keepdims=True
    )
    send_x[...] = mm(select, tok[...], NN).reshape(groups, cap, features).astype(BF16)

    pl.semaphore_wait(barrier, groups - 1 + reps - 1)

    def weight_copy(a, c, j):
        peer = lax.rem(rep + j, reps)
        src, dst = (
            (wg, full_g), (wu, full_u), (wd, full_d)
        )[a]
        if a < 2:
            src, dst = src.at[:, cols(c)], dst.at[mine, cols(c)]
        else:
            src, dst = src.at[cols(c), :], dst.at[cols(c), mine]
        return pltpu.make_async_remote_copy(
            src_ref=src, dst_ref=dst,
            send_sem=w_send.at[j - 1, a, c], recv_sem=w_recv.at[j - 1, a, c],
            device_id=(peer, exp), device_id_type=MESH,
        )

    def grad_copy(a, c, j):
        peer = lax.rem(rep + j, reps)
        theirs = pl.ds(pl.multiple_of(peer * share, share), share)
        src, dst = ((part_g, red_g), (part_u, red_u), (part_d, red_d))[a]
        if a < 2:
            src, dst = src.at[theirs, cols(c)], dst.at[j - 1, :, cols(c)]
        else:
            src, dst = src.at[cols(c), theirs], dst.at[j - 1, cols(c), :]
        return pltpu.make_async_remote_copy(
            src_ref=src, dst_ref=dst,
            send_sem=g_send.at[j - 1, a, c], recv_sem=g_recv.at[j - 1, a, c],
            device_id=(peer, exp), device_id_type=MESH,
        )

    exchange = ((send_x, recv_x), (send_c, recv_c), (send_o, recv_o), (send_d, recv_d))

    def row_copy(kind, i):
        peer = lax.rem(exp + i, groups)
        src, dst = exchange[kind]
        return pltpu.make_async_remote_copy(
            src_ref=src.at[peer], dst_ref=dst.at[exp],
            send_sem=a_send.at[kind, i - 1], recv_sem=a_recv.at[kind, i - 1],
            device_id=(rep, peer), device_id_type=MESH,
        )

    def start_rows(kind):
        def step(i, carry):
            row_copy(kind, i).start()
            return carry

        lax.fori_loop(1, groups, step, 0)
        src, dst = exchange[kind]
        pltpu.make_async_copy(src.at[exp], dst.at[exp], local_sem.at[3 + kind]).start()

    def finish_rows(kind):
        def step(i, carry):
            row_copy(kind, i).wait_recv()
            return carry

        lax.fori_loop(1, groups, step, 0)
        src, dst = exchange[kind]
        pltpu.make_async_copy(src.at[exp], dst.at[exp], local_sem.at[3 + kind]).wait()

    for c in range(chunks):
        for a in range(3):
            for j in range(1, reps):
                weight_copy(a, c, j).start()
    start_rows(0)
    send_c[...] = (
        (mm(select, cot[...], NN) * row_weight).reshape(groups, cap, features).astype(BF16)
    )
    start_rows(1)

    across = lax.broadcasted_iota(jnp.int32, (tokens, rows), 1).astype(F32)
    at0 = (across == dest[0]).astype(F32)
    at1 = (across == dest[1]).astype(F32)
    pick[...] = (at0 + at1).astype(BF16)
    weighted = at0 * cw_val[:, 0:1] + at1 * cw_val[:, 1:2]
    high = weighted.astype(BF16)
    pick_hi[...] = high
    pick_lo[...] = (weighted - high.astype(F32)).astype(BF16)

    for copy in own_copies:
        copy.wait()
    finish_rows(0)
    finish_rows(1)

    def chunk(c, carry):
        x = rows_2d(recv_x[...])
        for j in range(1, reps):
            for a in range(3):
                weight_copy(a, c, j).wait_recv()
        gate = mm(x, full_g[:, cols(c)], NN)
        up = mm(x, full_u[:, cols(c)], NN)
        cots = rows_2d(recv_c[...])
        grad_h = mm(cots, full_d[cols(c), :], NT)
        sigma = jax.nn.sigmoid(gate)
        swish = gate * sigma
        h = (swish * up).astype(BF16)
        dg = (grad_h * up * sigma * (1.0 + gate * (1.0 - sigma))).astype(BF16)
        du = (grad_h * swish).astype(BF16)
        hid[:, cols(c)] = h
        d_gate[:, cols(c)] = dg
        d_up[:, cols(c)] = du
        part_g[:, cols(c)] = mm(x, dg, TN).astype(BF16)
        for j in range(1, reps):
            grad_copy(0, c, j).start()
        part_u[:, cols(c)] = mm(x, du, TN).astype(BF16)
        for j in range(1, reps):
            grad_copy(1, c, j).start()
        part_d[cols(c), :] = mm(h, cots, TN).astype(BF16)
        for j in range(1, reps):
            grad_copy(2, c, j).start()
        return carry

    lax.fori_loop(0, chunks, chunk, 0)

    send_o[...] = mm(hid[...], full_d[...], NN).reshape(groups, cap, features).astype(BF16)
    start_rows(2)
    send_d[...] = (
        (mm(d_gate[...], full_g[...], NT) + mm(d_up[...], full_u[...], NT))
        .reshape(groups, cap, features)
        .astype(BF16)
    )
    start_rows(3)

    finish_rows(2)
    back = rows_2d(recv_o[...])
    mixed[...] = (mm(pick_hi[...], back, NN) + mm(pick_lo[...], back, NN)).astype(BF16)
    finish_rows(3)
    token_grad[...] = mm(pick[...], rows_2d(recv_d[...]), NN).astype(BF16)

    for c in range(chunks):
        for a in range(3):
            for j in range(1, reps):
                grad_copy(a, c, j).wait_recv()
            own, red, out = (
                (part_g, red_g, gate_grad), (part_u, red_u, up_grad), (part_d, red_d, down_grad)
            )[a]
            if a < 2:
                total = own[mine, cols(c)].astype(F32)
                for j in range(1, reps):
                    total = total + red[j - 1, :, cols(c)].astype(F32)
                out[:, cols(c)] = (total / reps).astype(BF16)
            else:
                total = own[cols(c), mine].astype(F32)
                for j in range(1, reps):
                    total = total + red[j - 1, cols(c), :].astype(F32)
                out[cols(c), :] = (total / reps).astype(BF16)

    for c in range(chunks):
        for a in range(3):
            for j in range(1, reps):
                weight_copy(a, c, j).wait_send()
                grad_copy(a, c, j).wait_send()

    def sent(i, carry):
        for kind in range(4):
            row_copy(kind, i).wait_send()
        return carry

    lax.fori_loop(1, groups, sent, 0)


def per_device(reps, groups, tokens, cotangent, expert_ids, combine_weight, gate_w, up_w, down_w):
    tok_rows, features = tokens.shape
    top = expert_ids.shape[1]
    share, hidden = gate_w.shape[1:]
    cap = 2 * tok_rows * top // groups
    rows = groups * cap
    width = 256
    chunks = hidden // width
    vmem = pl.BlockSpec(memory_space=pltpu.VMEM)
    block = pltpu.VMEM((groups, cap, features), BF16)
    act = pltpu.VMEM((rows, hidden), BF16)
    dma = pltpu.SemaphoreType.DMA
    others = reps - 1
    outs = pl.pallas_call(
        functools.partial(kernel, reps, groups, cap, width),
        out_shape=(
            jax.ShapeDtypeStruct((tok_rows, features), BF16),
            jax.ShapeDtypeStruct((tok_rows, features), BF16),
            jax.ShapeDtypeStruct((share, hidden), BF16),
            jax.ShapeDtypeStruct((share, hidden), BF16),
            jax.ShapeDtypeStruct((hidden, share), BF16),
        ),
        in_specs=[vmem] * 7,
        out_specs=(vmem,) * 5,
        scratch_shapes=[block] * 8
        + [
            pltpu.VMEM((features, hidden), BF16),
            pltpu.VMEM((features, hidden), BF16),
            pltpu.VMEM((hidden, features), BF16),
        ]
        + [act] * 3
        + [
            pltpu.VMEM((features, hidden), BF16),
            pltpu.VMEM((features, hidden), BF16),
            pltpu.VMEM((hidden, features), BF16),
            pltpu.VMEM((others, share, hidden), BF16),
            pltpu.VMEM((others, share, hidden), BF16),
            pltpu.VMEM((others, hidden, share), BF16),
        ]
        + [pltpu.VMEM((tok_rows, rows), BF16)] * 3
        + [
            dma((4, groups - 1)),
            dma((4, groups - 1)),
            dma((others, 3, chunks)),
            dma((others, 3, chunks)),
            dma((others, 3, chunks)),
            dma((others, 3, chunks)),
            dma((7,)),
        ],
        compiler_params=pltpu.CompilerParams(
            collective_id=0, has_side_effects=True, vmem_limit_bytes=56 * 1024 * 1024
        ),
        cost_estimate=pl.CostEstimate(
            flops=18 * rows * features * hidden,
            bytes_accessed=16 * share * hidden,
            transcendentals=rows * hidden,
        ),
    )(tokens, cotangent, expert_ids, combine_weight, gate_w[0], up_w[0], down_w[0])
    mixed, token_grad, gate_grad, up_grad, down_grad = outs
    return mixed, token_grad, gate_grad[None], up_grad[None], down_grad[None]


def solution(mesh):
    placed = (
        P(("rep", "exp"), None),
        P(("rep", "exp"), None),
        P(("rep", "exp"), None),
        P(("rep", "exp"), None),
        P("exp", "rep", None),
        P("exp", "rep", None),
        P("exp", None, "rep"),
    )
    return jax.shard_map(
        functools.partial(per_device, mesh.shape["rep"], mesh.shape["exp"]),
        mesh=mesh,
        in_specs=placed,
        out_specs=(
            P(("rep", "exp"), None),
            P(("rep", "exp"), None),
            P("exp", "rep", None),
            P("exp", "rep", None),
            P("exp", None, "rep"),
        ),
        check_vma=False,
    )
```

```python
import functools

import jax
import jax.numpy as jnp
from jax import lax
from jax.experimental import pallas as pl
from jax.experimental.pallas import tpu as pltpu
from jax.sharding import PartitionSpec as P

MESH = pl.DeviceIdType.MESH
F32, BF16 = jnp.float32, jnp.bfloat16
NN = (((1,), (0,)), ((), ()))
NT = (((1,), (1,)), ((), ()))
TN = (((0,), (0,)), ((), ()))


def mm(a, b, dims):
    return lax.dot_general(a, b, dims, preferred_element_type=F32)


def rows_2d(block):
    groups, capacity, features = block.shape
    if capacity % 16:
        return block.astype(F32).reshape(groups * capacity, features).astype(BF16)
    return block.reshape(groups * capacity, features)


def kernel(
    reps, groups, cap, width,
    tok, cot, ids, cw, wg, wu, wd,
    out_mixed, out_tokens, out_gate, out_up, out_down,
    send_x, send_c, send_o, send_d, recv_x, recv_c, recv_o, recv_d,
    full_g, full_u, full_d, hid, d_gate, d_up,
    part_g, part_u, part_d, red_g, red_u, red_d,
    pick, pick_hi, pick_lo,
    flip_x, slope_g, slope_u, mixed, token_grad, gate_grad, up_grad, down_grad,
    a_send, a_recv, w_send, w_recv, g_send, g_recv, local_sem, out_sem,
):
    rep, exp = lax.axis_index("rep"), lax.axis_index("exp")
    tokens, features = tok.shape
    share, hidden = wg.shape
    chunks = hidden // width
    last = chunks - 1
    rows = groups * cap
    mine = pl.ds(pl.multiple_of(rep * share, share), share)

    def cols(c):
        if isinstance(c, int):
            return pl.ds(c * width, width)
        return pl.ds(pl.multiple_of(c * width, width), width)

    barrier = pltpu.get_barrier_semaphore()
    for j in range(1, reps):
        pl.semaphore_signal(
            barrier, inc=1, device_id=(lax.rem(rep + j, reps), exp), device_id_type=MESH
        )

    def greet(i, carry):
        pl.semaphore_signal(
            barrier, inc=1, device_id=(rep, lax.rem(exp + i, groups)), device_id_type=MESH
        )
        return carry

    lax.fori_loop(1, groups, greet, 0)

    own_copies = [
        pltpu.make_async_copy(wg, full_g.at[mine, :], local_sem.at[0]),
        pltpu.make_async_copy(wu, full_u.at[mine, :], local_sem.at[1]),
        pltpu.make_async_copy(wd, full_d.at[:, mine], local_sem.at[2]),
    ]
    for copy in own_copies:
        copy.start()

    lanes = 128
    expert = lax.broadcasted_iota(jnp.int32, (lanes, tokens), 0)
    id_val = ids[...]
    cw_val = cw[...]
    hot = [(id_val[k : k + 1, :] == expert).astype(F32) for k in range(2)]
    earlier = (
        lax.broadcasted_iota(jnp.int32, (tokens, tokens), 0)
        < lax.broadcasted_iota(jnp.int32, (tokens, tokens), 1)
    )
    before = mm((hot[0] + hot[1]).astype(BF16), earlier.astype(F32).astype(BF16), NN)
    place = before + (expert * cap).astype(F32)
    dest = [jnp.sum(hot[k] * place, axis=0, keepdims=True) for k in range(2)]
    down_rows = lax.broadcasted_iota(jnp.int32, (rows, tokens), 0).astype(F32)
    sel0 = (down_rows == dest[0]).astype(F32)
    sel1 = (down_rows == dest[1]).astype(F32)
    select = (sel0 + sel1).astype(BF16)

    pl.semaphore_wait(barrier, groups - 1 + reps - 1)

    def weight_copy(a, c, j):
        peer = lax.rem(rep + j, reps)
        src, dst = (
            (wg, full_g), (wu, full_u), (wd, full_d)
        )[a]
        if a < 2:
            src, dst = src.at[:, cols(c)], dst.at[mine, cols(c)]
        else:
            src, dst = src.at[cols(c), :], dst.at[cols(c), mine]
        return pltpu.make_async_remote_copy(
            src_ref=src, dst_ref=dst,
            send_sem=w_send.at[j - 1, a, c], recv_sem=w_recv.at[j - 1, a, c],
            device_id=(peer, exp), device_id_type=MESH,
        )

    def grad_copy(a, c, j):
        peer = lax.rem(rep + j, reps)
        theirs = pl.ds(pl.multiple_of(peer * share, share), share)
        src, dst = ((part_g, red_g), (part_u, red_u), (part_d, red_d))[a]
        if a < 2:
            src, dst = src.at[theirs, cols(c)], dst.at[j - 1, :, cols(c)]
        else:
            src, dst = src.at[cols(c), theirs], dst.at[j - 1, cols(c), :]
        return pltpu.make_async_remote_copy(
            src_ref=src, dst_ref=dst,
            send_sem=g_send.at[j - 1, a, c], recv_sem=g_recv.at[j - 1, a, c],
            device_id=(peer, exp), device_id_type=MESH,
        )

    exchange = ((send_x, recv_x), (send_c, recv_c), (send_o, recv_o), (send_d, recv_d))

    def row_copy(kind, i):
        peer = lax.rem(exp + i, groups)
        src, dst = exchange[kind]
        return pltpu.make_async_remote_copy(
            src_ref=src.at[peer], dst_ref=dst.at[exp],
            send_sem=a_send.at[kind, i - 1], recv_sem=a_recv.at[kind, i - 1],
            device_id=(rep, peer), device_id_type=MESH,
        )

    def start_rows(kind):
        def step(k, carry):
            i = groups // 2 + (1 - 2 * lax.rem(k, 2)) * ((k + 1) // 2)
            row_copy(kind, i).start()
            return carry

        lax.fori_loop(0, groups - 1, step, 0)
        src, dst = exchange[kind]
        pltpu.make_async_copy(src.at[exp], dst.at[exp], local_sem.at[3 + kind]).start()

    def finish_rows(kind):
        def step(i, carry):
            row_copy(kind, i).wait_recv()
            return carry

        lax.fori_loop(1, groups, step, 0)
        src, dst = exchange[kind]
        pltpu.make_async_copy(src.at[exp], dst.at[exp], local_sem.at[3 + kind]).wait()

    for c in range(chunks):
        for a in range(2):
            for j in range(1, reps):
                weight_copy(a, c, j).start()
    for c in range(chunks):
        for j in range(1, reps):
            weight_copy(2, c, j).start()
    send_x[...] = mm(select, tok[...], NN).reshape(groups, cap, features).astype(BF16)
    start_rows(0)
    row_weight = jnp.sum(
        sel0 * cw_val[0:1, :] + sel1 * cw_val[1:2, :], axis=1, keepdims=True
    )
    send_c[...] = (
        (mm(select, cot[...], NN) * row_weight).reshape(groups, cap, features).astype(BF16)
    )
    start_rows(1)

    table = jnp.where(
        expert == 0, dest[0],
        jnp.where(expert == 1, dest[1],
                  jnp.where(expert == 2, cw_val[0:1, :],
                            jnp.where(expert == 3, cw_val[1:2, :], 0.0))),
    )
    flipped = jnp.transpose(table)
    across = lax.broadcasted_iota(jnp.int32, (tokens, rows), 1).astype(F32)
    at0 = (across == flipped[:, 0:1]).astype(F32)
    at1 = (across == flipped[:, 1:2]).astype(F32)
    pick[...] = (at0 + at1).astype(BF16)
    weighted = at0 * flipped[:, 2:3] + at1 * flipped[:, 3:4]
    high = weighted.astype(BF16)
    pick_hi[...] = high
    pick_lo[...] = (weighted - high.astype(F32)).astype(BF16)

    for copy in own_copies:
        copy.wait()
    finish_rows(0)
    flip_x[...] = jnp.transpose(rows_2d(recv_x[...]))

    def forward(c, carry):
        x = rows_2d(recv_x[...])
        for j in range(1, reps):
            weight_copy(0, c, j).wait_recv()
        gate = mm(x, full_g[:, cols(c)], NN)
        for j in range(1, reps):
            weight_copy(1, c, j).wait_recv()
        up = mm(x, full_u[:, cols(c)], NN)
        sigma = jax.nn.sigmoid(gate)
        swish = gate * sigma
        hid[:, cols(c)] = (swish * up).astype(BF16)
        slope_u[:, cols(c)] = swish
        slope_g[:, cols(c)] = up * sigma * (1.0 + gate * (1.0 - sigma))
        return carry

    def backward(c):
        grad_h = mm(rows_2d(recv_c[...]), full_d[cols(c), :], NT)
        d_gate[:, cols(c)] = (grad_h * slope_g[:, cols(c)]).astype(BF16)
        d_up[:, cols(c)] = (grad_h * slope_u[:, cols(c)]).astype(BF16)

    def gradients(c, carry):
        part_g[:, cols(c)] = mm(flip_x[...], d_gate[:, cols(c)], NN).astype(BF16)
        for j in range(1, reps):
            grad_copy(0, c, j).start()
        part_u[:, cols(c)] = mm(flip_x[...], d_up[:, cols(c)], NN).astype(BF16)
        for j in range(1, reps):
            grad_copy(1, c, j).start()
        part_d[cols(c), :] = mm(hid[:, cols(c)], rows_2d(recv_c[...]), TN).astype(BF16)
        for j in range(1, reps):
            grad_copy(2, c, j).start()
        return carry

    lax.fori_loop(0, chunks, forward, 0)
    finish_rows(1)
    for c in range(chunks):
        for j in range(1, reps):
            weight_copy(2, c, j).wait_recv()
        if c == last:
            send_o[...] = (
                mm(hid[...], full_d[...], NN).reshape(groups, cap, features).astype(BF16)
            )
            start_rows(2)
        backward(c)
        if c == 0 and last > 0:
            gradients(0, 0)
    send_d[...] = (
        (mm(d_gate[...], full_g[...], NT) + mm(d_up[...], full_u[...], NT))
        .reshape(groups, cap, features)
        .astype(BF16)
    )
    start_rows(3)
    lax.fori_loop(min(1, last), chunks, gradients, 0)

    writes = []

    def write(src, dst):
        copy = pltpu.make_async_copy(src, dst, out_sem.at[len(writes)])
        copy.start()
        writes.append(copy)

    def average(c):
        for a in range(3):
            for j in range(1, reps):
                grad_copy(a, c, j).wait_recv()
            own, red, mean, out = (
                (part_g, red_g, gate_grad, out_gate),
                (part_u, red_u, up_grad, out_up),
                (part_d, red_d, down_grad, out_down),
            )[a]
            here, there = ((slice(None), cols(c)), (mine, cols(c)))
            if a == 2:
                here, there = ((cols(c), slice(None)), (cols(c), mine))
            total = own[there].astype(F32)
            for j in range(1, reps):
                total = total + red[(j - 1,) + here].astype(F32)
            mean[here] = (total / reps).astype(BF16)
            write(mean.at[here], out.at[here])

    finish_rows(2)
    back = rows_2d(recv_o[...])
    mixed[...] = (mm(pick_hi[...], back, NN) + mm(pick_lo[...], back, NN)).astype(BF16)
    write(mixed, out_mixed)
    for c in range(last):
        average(c)
    finish_rows(3)
    token_grad[...] = mm(pick[...], rows_2d(recv_d[...]), NN).astype(BF16)
    write(token_grad, out_tokens)
    average(last)

    for c in range(chunks):
        for a in range(3):
            for j in range(1, reps):
                weight_copy(a, c, j).wait_send()
                grad_copy(a, c, j).wait_send()

    def sent(i, carry):
        for kind in range(4):
            row_copy(kind, i).wait_send()
        return carry

    lax.fori_loop(1, groups, sent, 0)
    for copy in writes:
        copy.wait()


def hand_out(count, *refs):
    sems = refs[-1]
    copies = [
        pltpu.make_async_copy(refs[k], refs[count + k], sems.at[k]) for k in range(count)
    ]
    for copy in copies:
        copy.start()
    for copy in copies:
        copy.wait()


def per_device(reps, groups, tokens, cotangent, expert_ids, combine_weight, gate_w, up_w, down_w):
    tok_rows, features = tokens.shape
    top = expert_ids.shape[1]
    share, hidden = gate_w.shape[1:]
    cap = 2 * tok_rows * top // groups
    rows = groups * cap
    width = 256
    chunks = hidden // width
    vmem = pl.BlockSpec(memory_space=pltpu.VMEM)
    anywhere = pl.BlockSpec(memory_space=pl.ANY)
    block = pltpu.VMEM((groups, cap, features), BF16)
    act = pltpu.VMEM((rows, hidden), BF16)
    dma = pltpu.SemaphoreType.DMA
    others = reps - 1
    shapes = (
        jax.ShapeDtypeStruct((tok_rows, features), BF16),
        jax.ShapeDtypeStruct((tok_rows, features), BF16),
        jax.ShapeDtypeStruct((share, hidden), BF16),
        jax.ShapeDtypeStruct((share, hidden), BF16),
        jax.ShapeDtypeStruct((hidden, share), BF16),
    )
    outs = pl.pallas_call(
        functools.partial(kernel, reps, groups, cap, width),
        out_shape=shapes,
        in_specs=[vmem] * 4 + [anywhere] * 3,
        out_specs=(anywhere,) * 5,
        scratch_shapes=[block] * 8
        + [
            pltpu.VMEM((features, hidden), BF16),
            pltpu.VMEM((features, hidden), BF16),
            pltpu.VMEM((hidden, features), BF16),
        ]
        + [act] * 3
        + [
            pltpu.VMEM((features, hidden), BF16),
            pltpu.VMEM((features, hidden), BF16),
            pltpu.VMEM((hidden, features), BF16),
            pltpu.VMEM((others, share, hidden), BF16),
            pltpu.VMEM((others, share, hidden), BF16),
            pltpu.VMEM((others, hidden, share), BF16),
        ]
        + [pltpu.VMEM((tok_rows, rows), BF16)] * 3
        + [pltpu.VMEM((features, rows), BF16)]
        + [pltpu.VMEM((rows, hidden), F32)] * 2
        + [pltpu.VMEM(shape.shape, BF16) for shape in shapes]
        + [
            dma((4, groups - 1)),
            dma((4, groups - 1)),
            dma((others, 3, chunks)),
            dma((others, 3, chunks)),
            dma((others, 3, chunks)),
            dma((others, 3, chunks)),
            dma((7,)),
            dma((2 + 3 * chunks,)),
        ],
        compiler_params=pltpu.CompilerParams(
            collective_id=0, has_side_effects=True, vmem_limit_bytes=56 * 1024 * 1024
        ),
        cost_estimate=pl.CostEstimate(
            flops=18 * rows * features * hidden,
            bytes_accessed=16 * share * hidden,
            transcendentals=rows * hidden,
        ),
    )(tokens, cotangent, expert_ids.T, combine_weight.T, gate_w[0], up_w[0], down_w[0])
    mixed, token_grad, gate_grad, up_grad, down_grad = pl.pallas_call(
        functools.partial(hand_out, len(shapes)),
        out_shape=shapes,
        in_specs=[anywhere] * len(shapes),
        out_specs=(anywhere,) * len(shapes),
        scratch_shapes=[dma((len(shapes),))],
        compiler_params=pltpu.CompilerParams(vmem_limit_bytes=60 * 1024 * 1024),
    )(*outs)
    return mixed, token_grad, gate_grad[None], up_grad[None], down_grad[None]


def solution(mesh):
    placed = (
        P(("rep", "exp"), None),
        P(("rep", "exp"), None),
        P(("rep", "exp"), None),
        P(("rep", "exp"), None),
        P("exp", "rep", None),
        P("exp", "rep", None),
        P("exp", None, "rep"),
    )
    return jax.shard_map(
        functools.partial(per_device, mesh.shape["rep"], mesh.shape["exp"]),
        mesh=mesh,
        in_specs=placed,
        out_specs=(
            P(("rep", "exp"), None),
            P(("rep", "exp"), None),
            P("exp", "rep", None),
            P("exp", "rep", None),
            P("exp", None, "rep"),
        ),
        check_vma=False,
    )
```

```python
import functools

import jax
import jax.numpy as jnp
from jax import lax
from jax.experimental import pallas as pl
from jax.experimental.pallas import tpu as pltpu
from jax.sharding import PartitionSpec as P

MESH = pl.DeviceIdType.MESH
F32, BF16 = jnp.float32, jnp.bfloat16
NN = (((1,), (0,)), ((), ()))
NT = (((1,), (1,)), ((), ()))
TN = (((0,), (0,)), ((), ()))


def mm(a, b, dims):
    return lax.dot_general(a, b, dims, preferred_element_type=F32)


def rows_2d(block):
    groups, capacity, features = block.shape
    if capacity % 16:
        return block.astype(F32).reshape(groups * capacity, features).astype(BF16)
    return block.reshape(groups * capacity, features)


def kernel(
    reps, groups, cap, width,
    tok, cot, ids, cw, wg, wu, wd,
    out_mixed, out_tokens, out_gate, out_up, out_down,
    send_x, send_c, send_o, send_d, recv_x, recv_c, recv_o, recv_d,
    full_g, full_u, full_d, hid, d_gate, d_up,
    part_g, part_u, part_d, red_g, red_u, red_d,
    pick, pick_hi, pick_lo,
    flip_x, slope_g, slope_u, mixed, token_grad, gate_grad, up_grad, down_grad,
    a_send, a_recv, w_send, w_recv, g_send, g_recv, local_sem, out_sem,
):
    rep, exp = lax.axis_index("rep"), lax.axis_index("exp")
    tokens, features = tok.shape
    share, hidden = wg.shape
    chunks = hidden // width
    last = chunks - 1
    rows = groups * cap
    mine = pl.ds(pl.multiple_of(rep * share, share), share)

    def cols(c):
        if isinstance(c, int):
            return pl.ds(c * width, width)
        return pl.ds(pl.multiple_of(c * width, width), width)

    barrier = pltpu.get_barrier_semaphore()
    for j in range(1, reps):
        pl.semaphore_signal(
            barrier, inc=1, device_id=(lax.rem(rep + j, reps), exp), device_id_type=MESH
        )

    def greet(i, carry):
        pl.semaphore_signal(
            barrier, inc=1, device_id=(rep, lax.rem(exp + i, groups)), device_id_type=MESH
        )
        return carry

    lax.fori_loop(1, groups, greet, 0)

    own_copies = [
        pltpu.make_async_copy(wg, full_g.at[mine, :], local_sem.at[0]),
        pltpu.make_async_copy(wu, full_u.at[mine, :], local_sem.at[1]),
        pltpu.make_async_copy(wd, full_d.at[:, mine], local_sem.at[2]),
    ]
    for copy in own_copies:
        copy.start()

    lanes = 128
    expert = lax.broadcasted_iota(jnp.int32, (lanes, tokens), 0)
    id_val = ids[...]
    cw_val = cw[...]
    hot = [(id_val[k : k + 1, :] == expert).astype(F32) for k in range(2)]
    earlier = (
        lax.broadcasted_iota(jnp.int32, (tokens, tokens), 0)
        < lax.broadcasted_iota(jnp.int32, (tokens, tokens), 1)
    )
    before = mm((hot[0] + hot[1]).astype(BF16), earlier.astype(F32).astype(BF16), NN)
    place = before + (expert * cap).astype(F32)
    dest = [jnp.sum(hot[k] * place, axis=0, keepdims=True) for k in range(2)]
    down_rows = lax.broadcasted_iota(jnp.int32, (rows, tokens), 0).astype(F32)
    sel0 = (down_rows == dest[0]).astype(F32)
    sel1 = (down_rows == dest[1]).astype(F32)
    select = (sel0 + sel1).astype(BF16)

    pl.semaphore_wait(barrier, groups - 1 + reps - 1)

    def weight_copy(a, c, j):
        peer = lax.rem(rep + j, reps)
        src, dst = (
            (wg, full_g), (wu, full_u), (wd, full_d)
        )[a]
        if a < 2:
            src, dst = src.at[:, cols(c)], dst.at[mine, cols(c)]
        else:
            src, dst = src.at[cols(c), :], dst.at[cols(c), mine]
        return pltpu.make_async_remote_copy(
            src_ref=src, dst_ref=dst,
            send_sem=w_send.at[j - 1, a, c], recv_sem=w_recv.at[j - 1, a, c],
            device_id=(peer, exp), device_id_type=MESH,
        )

    def grad_copy(a, c, j):
        peer = lax.rem(rep + j, reps)
        theirs = pl.ds(pl.multiple_of(peer * share, share), share)
        src, dst = ((part_g, red_g), (part_u, red_u), (part_d, red_d))[a]
        if a < 2:
            src, dst = src.at[theirs, cols(c)], dst.at[j - 1, :, cols(c)]
        else:
            src, dst = src.at[cols(c), theirs], dst.at[j - 1, cols(c), :]
        return pltpu.make_async_remote_copy(
            src_ref=src, dst_ref=dst,
            send_sem=g_send.at[j - 1, a, c], recv_sem=g_recv.at[j - 1, a, c],
            device_id=(peer, exp), device_id_type=MESH,
        )

    exchange = ((send_x, recv_x), (send_c, recv_c), (send_o, recv_o), (send_d, recv_d))

    def row_copy(kind, i):
        peer = lax.rem(exp + i, groups)
        src, dst = exchange[kind]
        return pltpu.make_async_remote_copy(
            src_ref=src.at[peer], dst_ref=dst.at[exp],
            send_sem=a_send.at[kind, i - 1], recv_sem=a_recv.at[kind, i - 1],
            device_id=(rep, peer), device_id_type=MESH,
        )

    def start_rows(kind):
        def step(k, carry):
            i = groups // 2 + (1 - 2 * lax.rem(k, 2)) * ((k + 1) // 2)
            row_copy(kind, i).start()
            return carry

        lax.fori_loop(0, groups - 1, step, 0)
        src, dst = exchange[kind]
        pltpu.make_async_copy(src.at[exp], dst.at[exp], local_sem.at[3 + kind]).start()

    def finish_rows(kind):
        def step(i, carry):
            row_copy(kind, i).wait_recv()
            return carry

        lax.fori_loop(1, groups, step, 0)
        src, dst = exchange[kind]
        pltpu.make_async_copy(src.at[exp], dst.at[exp], local_sem.at[3 + kind]).wait()

    for c in range(chunks):
        for a in range(2):
            for j in range(1, reps):
                weight_copy(a, c, j).start()
    for c in range(chunks):
        for j in range(1, reps):
            weight_copy(2, c, j).start()
    send_x[...] = mm(select, tok[...], NN).reshape(groups, cap, features).astype(BF16)
    start_rows(0)
    row_weight = jnp.sum(
        sel0 * cw_val[0:1, :] + sel1 * cw_val[1:2, :], axis=1, keepdims=True
    )
    send_c[...] = (
        (mm(select, cot[...], NN) * row_weight).reshape(groups, cap, features).astype(BF16)
    )
    start_rows(1)

    table = jnp.where(
        expert == 0, dest[0],
        jnp.where(expert == 1, dest[1],
                  jnp.where(expert == 2, cw_val[0:1, :],
                            jnp.where(expert == 3, cw_val[1:2, :], 0.0))),
    )
    flipped = jnp.transpose(table)
    across = lax.broadcasted_iota(jnp.int32, (tokens, rows), 1).astype(F32)
    at0 = (across == flipped[:, 0:1]).astype(F32)
    at1 = (across == flipped[:, 1:2]).astype(F32)
    pick[...] = (at0 + at1).astype(BF16)
    weighted = at0 * flipped[:, 2:3] + at1 * flipped[:, 3:4]
    high = weighted.astype(BF16)
    pick_hi[...] = high
    pick_lo[...] = (weighted - high.astype(F32)).astype(BF16)

    for copy in own_copies:
        copy.wait()
    finish_rows(0)
    flip_x[...] = jnp.transpose(rows_2d(recv_x[...]))

    def forward(c, carry):
        x = rows_2d(recv_x[...])
        for j in range(1, reps):
            weight_copy(0, c, j).wait_recv()
        gate = mm(x, full_g[:, cols(c)], NN)
        for j in range(1, reps):
            weight_copy(1, c, j).wait_recv()
        up = mm(x, full_u[:, cols(c)], NN)
        sigma = jax.nn.sigmoid(gate)
        swish = gate * sigma
        hid[:, cols(c)] = (swish * up).astype(BF16)
        slope_u[:, cols(c)] = swish
        slope_g[:, cols(c)] = up * sigma * (1.0 + gate * (1.0 - sigma))
        return carry

    def backward(c):
        grad_h = mm(rows_2d(recv_c[...]), full_d[cols(c), :], NT)
        d_gate[:, cols(c)] = (grad_h * slope_g[:, cols(c)]).astype(BF16)
        d_up[:, cols(c)] = (grad_h * slope_u[:, cols(c)]).astype(BF16)

    def gradients(c, carry):
        part_g[:, cols(c)] = mm(flip_x[...], d_gate[:, cols(c)], NN).astype(BF16)
        for j in range(1, reps):
            grad_copy(0, c, j).start()
        part_u[:, cols(c)] = mm(flip_x[...], d_up[:, cols(c)], NN).astype(BF16)
        for j in range(1, reps):
            grad_copy(1, c, j).start()
        part_d[cols(c), :] = mm(hid[:, cols(c)], rows_2d(recv_c[...]), TN).astype(BF16)
        for j in range(1, reps):
            grad_copy(2, c, j).start()
        return carry

    lax.fori_loop(0, chunks, forward, 0)
    finish_rows(1)
    for c in range(chunks):
        for j in range(1, reps):
            weight_copy(2, c, j).wait_recv()
        if c == last:
            send_o[...] = (
                mm(hid[...], full_d[...], NN).reshape(groups, cap, features).astype(BF16)
            )
            start_rows(2)
        backward(c)
        if c == 0 and last > 0:
            gradients(0, 0)
    send_d[...] = (
        (mm(d_gate[...], full_g[...], NT) + mm(d_up[...], full_u[...], NT))
        .reshape(groups, cap, features)
        .astype(BF16)
    )
    start_rows(3)
    lax.fori_loop(min(1, last), chunks, gradients, 0)

    writes = []

    def write(src, dst):
        copy = pltpu.make_async_copy(src, dst, out_sem.at[len(writes)])
        copy.start()
        writes.append(copy)

    def average(c):
        for a in range(3):
            for j in range(1, reps):
                grad_copy(a, c, j).wait_recv()
            own, red, mean, out = (
                (part_g, red_g, gate_grad, out_gate),
                (part_u, red_u, up_grad, out_up),
                (part_d, red_d, down_grad, out_down),
            )[a]
            here, there = ((slice(None), cols(c)), (mine, cols(c)))
            if a == 2:
                here, there = ((cols(c), slice(None)), (cols(c), mine))
            total = own[there].astype(F32)
            for j in range(1, reps):
                total = total + red[(j - 1,) + here].astype(F32)
            mean[here] = (total / reps).astype(BF16)
            write(mean.at[here], out.at[here])

    finish_rows(2)
    back = rows_2d(recv_o[...])
    mixed[...] = (mm(pick_hi[...], back, NN) + mm(pick_lo[...], back, NN)).astype(BF16)
    write(mixed, out_mixed)
    for c in range(last):
        average(c)
    finish_rows(3)
    token_grad[...] = mm(pick[...], rows_2d(recv_d[...]), NN).astype(BF16)
    write(token_grad, out_tokens)
    average(last)

    for c in range(chunks):
        for a in range(3):
            for j in range(1, reps):
                weight_copy(a, c, j).wait_send()
                grad_copy(a, c, j).wait_send()

    def sent(i, carry):
        for kind in range(4):
            row_copy(kind, i).wait_send()
        return carry

    lax.fori_loop(1, groups, sent, 0)
    for copy in writes:
        copy.wait()


def hand_out(count, *refs):
    sources, targets, stages = refs[:count], refs[count : 2 * count], refs[2 * count : 3 * count]
    sems = refs[-1]
    loads = [
        pltpu.make_async_copy(sources[k], stages[k], sems.at[0, k]) for k in range(count)
    ]
    stores = [
        pltpu.make_async_copy(stages[k], targets[k], sems.at[1, k]) for k in range(count)
    ]
    for load in loads:
        load.start()
    for load, store in zip(loads, stores):
        load.wait()
        store.start()
    for store in stores:
        store.wait()


def per_device(reps, groups, tokens, cotangent, expert_ids, combine_weight, gate_w, up_w, down_w):
    tok_rows, features = tokens.shape
    top = expert_ids.shape[1]
    share, hidden = gate_w.shape[1:]
    cap = 2 * tok_rows * top // groups
    rows = groups * cap
    width = 256
    chunks = hidden // width
    vmem = pl.BlockSpec(memory_space=pltpu.VMEM)
    anywhere = pl.BlockSpec(memory_space=pl.ANY)
    block = pltpu.VMEM((groups, cap, features), BF16)
    act = pltpu.VMEM((rows, hidden), BF16)
    dma = pltpu.SemaphoreType.DMA
    others = reps - 1
    shapes = (
        jax.ShapeDtypeStruct((tok_rows, features), BF16),
        jax.ShapeDtypeStruct((tok_rows, features), BF16),
        jax.ShapeDtypeStruct((share, hidden), BF16),
        jax.ShapeDtypeStruct((share, hidden), BF16),
        jax.ShapeDtypeStruct((hidden, share), BF16),
    )
    outs = pl.pallas_call(
        functools.partial(kernel, reps, groups, cap, width),
        out_shape=shapes,
        in_specs=[vmem] * 4 + [anywhere] * 3,
        out_specs=(anywhere,) * 5,
        scratch_shapes=[block] * 8
        + [
            pltpu.VMEM((features, hidden), BF16),
            pltpu.VMEM((features, hidden), BF16),
            pltpu.VMEM((hidden, features), BF16),
        ]
        + [act] * 3
        + [
            pltpu.VMEM((features, hidden), BF16),
            pltpu.VMEM((features, hidden), BF16),
            pltpu.VMEM((hidden, features), BF16),
            pltpu.VMEM((others, share, hidden), BF16),
            pltpu.VMEM((others, share, hidden), BF16),
            pltpu.VMEM((others, hidden, share), BF16),
        ]
        + [pltpu.VMEM((tok_rows, rows), BF16)] * 3
        + [pltpu.VMEM((features, rows), BF16)]
        + [pltpu.VMEM((rows, hidden), F32)] * 2
        + [pltpu.VMEM(shape.shape, BF16) for shape in shapes]
        + [
            dma((4, groups - 1)),
            dma((4, groups - 1)),
            dma((others, 3, chunks)),
            dma((others, 3, chunks)),
            dma((others, 3, chunks)),
            dma((others, 3, chunks)),
            dma((7,)),
            dma((2 + 3 * chunks,)),
        ],
        compiler_params=pltpu.CompilerParams(
            collective_id=0, has_side_effects=True, vmem_limit_bytes=56 * 1024 * 1024
        ),
        cost_estimate=pl.CostEstimate(
            flops=18 * rows * features * hidden,
            bytes_accessed=16 * share * hidden,
            transcendentals=rows * hidden,
        ),
    )(tokens, cotangent, expert_ids.T, combine_weight.T, gate_w[0], up_w[0], down_w[0])
    mixed, token_grad, gate_grad, up_grad, down_grad = pl.pallas_call(
        functools.partial(hand_out, len(shapes)),
        out_shape=shapes,
        in_specs=[anywhere] * len(shapes),
        out_specs=(anywhere,) * len(shapes),
        scratch_shapes=[pltpu.VMEM(shape.shape, BF16) for shape in shapes] + [dma((2, len(shapes)))],
        compiler_params=pltpu.CompilerParams(vmem_limit_bytes=60 * 1024 * 1024),
    )(*outs)
    return mixed, token_grad, gate_grad[None], up_grad[None], down_grad[None]


def solution(mesh):
    placed = (
        P(("rep", "exp"), None),
        P(("rep", "exp"), None),
        P(("rep", "exp"), None),
        P(("rep", "exp"), None),
        P("exp", "rep", None),
        P("exp", "rep", None),
        P("exp", None, "rep"),
    )
    return jax.shard_map(
        functools.partial(per_device, mesh.shape["rep"], mesh.shape["exp"]),
        mesh=mesh,
        in_specs=placed,
        out_specs=(
            P(("rep", "exp"), None),
            P(("rep", "exp"), None),
            P("exp", "rep", None),
            P("exp", "rep", None),
            P("exp", None, "rep"),
        ),
        check_vma=False,
    )
```

```python
import functools

import jax
import jax.numpy as jnp
from jax import lax
from jax.experimental import pallas as pl
from jax.experimental.pallas import tpu as pltpu
from jax.sharding import PartitionSpec as P

MESH = pl.DeviceIdType.MESH
F32, BF16 = jnp.float32, jnp.bfloat16
NN = (((1,), (0,)), ((), ()))
NT = (((1,), (1,)), ((), ()))
TN = (((0,), (0,)), ((), ()))


def mm(a, b, dims):
    return lax.dot_general(a, b, dims, preferred_element_type=F32)


def rows_2d(block):
    groups, capacity, features = block.shape
    if capacity % 16:
        return block.astype(F32).reshape(groups * capacity, features).astype(BF16)
    return block.reshape(groups * capacity, features)


def kernel(
    reps, groups, cap, width,
    tok_in, cot_in, ids_in, cw_in, wg, wu, wd,
    out_mixed, out_tokens, out_gate, out_up, out_down,
    send_x, send_c, send_o, send_d, recv_x, recv_c, recv_o, recv_d,
    full_g, full_u, full_d, hid, d_gate, d_up,
    part_g, part_u, part_d, red_g, red_u, red_d,
    pick, pick_hi, pick_lo,
    flip_x, slope_g, slope_u, mixed, token_grad, gate_grad, up_grad, down_grad,
    tok, cot, ids, cw,
    a_send, a_recv, w_send, w_recv, g_send, g_recv, local_sem, out_sem,
):
    rep, exp = lax.axis_index("rep"), lax.axis_index("exp")
    tokens, features = tok_in.shape
    share, hidden = wg.shape
    chunks = hidden // width
    last = chunks - 1
    rows = groups * cap
    mine = pl.ds(pl.multiple_of(rep * share, share), share)

    def cols(c):
        if isinstance(c, int):
            return pl.ds(c * width, width)
        return pl.ds(pl.multiple_of(c * width, width), width)

    barrier = pltpu.get_barrier_semaphore()
    for j in range(1, reps):
        pl.semaphore_signal(
            barrier, inc=1, device_id=(lax.rem(rep + j, reps), exp), device_id_type=MESH
        )

    def greet(i, carry):
        pl.semaphore_signal(
            barrier, inc=1, device_id=(rep, lax.rem(exp + i, groups)), device_id_type=MESH
        )
        return carry

    lax.fori_loop(1, groups, greet, 0)

    loads = [
        pltpu.make_async_copy(src, dst, local_sem.at[7 + k])
        for k, (src, dst) in enumerate(((ids_in, ids), (cw_in, cw), (tok_in, tok), (cot_in, cot)))
    ]
    for load in loads:
        load.start()
    pl.semaphore_wait(barrier, groups - 1 + reps - 1)

    def weight_copy(a, c, j):
        peer = lax.rem(rep + j, reps)
        src, dst = (
            (wg, full_g), (wu, full_u), (wd, full_d)
        )[a]
        if a < 2:
            src, dst = src.at[:, cols(c)], dst.at[mine, cols(c)]
        else:
            src, dst = src.at[cols(c), :], dst.at[cols(c), mine]
        return pltpu.make_async_remote_copy(
            src_ref=src, dst_ref=dst,
            send_sem=w_send.at[j - 1, a, c], recv_sem=w_recv.at[j - 1, a, c],
            device_id=(peer, exp), device_id_type=MESH,
        )

    for c in range(chunks):
        for a in range(2):
            for j in range(1, reps):
                weight_copy(a, c, j).start()
    for c in range(chunks):
        for j in range(1, reps):
            weight_copy(2, c, j).start()

    own_copies = [
        pltpu.make_async_copy(wg, full_g.at[mine, :], local_sem.at[0]),
        pltpu.make_async_copy(wu, full_u.at[mine, :], local_sem.at[1]),
        pltpu.make_async_copy(wd, full_d.at[:, mine], local_sem.at[2]),
    ]
    for copy in own_copies:
        copy.start()

    lanes = 128
    expert = lax.broadcasted_iota(jnp.int32, (lanes, tokens), 0)
    loads[0].wait()
    loads[1].wait()
    id_val = ids[...]
    cw_val = cw[...]
    hot = [(id_val[k : k + 1, :] == expert).astype(F32) for k in range(2)]
    earlier = (
        lax.broadcasted_iota(jnp.int32, (tokens, tokens), 0)
        < lax.broadcasted_iota(jnp.int32, (tokens, tokens), 1)
    )
    before = mm((hot[0] + hot[1]).astype(BF16), earlier.astype(F32).astype(BF16), NN)
    place = before + (expert * cap).astype(F32)
    dest = [jnp.sum(hot[k] * place, axis=0, keepdims=True) for k in range(2)]
    down_rows = lax.broadcasted_iota(jnp.int32, (rows, tokens), 0).astype(F32)
    sel0 = (down_rows == dest[0]).astype(F32)
    sel1 = (down_rows == dest[1]).astype(F32)
    select = (sel0 + sel1).astype(BF16)

    def grad_copy(a, c, j):
        peer = lax.rem(rep + j, reps)
        theirs = pl.ds(pl.multiple_of(peer * share, share), share)
        src, dst = ((part_g, red_g), (part_u, red_u), (part_d, red_d))[a]
        if a < 2:
            src, dst = src.at[theirs, cols(c)], dst.at[j - 1, :, cols(c)]
        else:
            src, dst = src.at[cols(c), theirs], dst.at[j - 1, cols(c), :]
        return pltpu.make_async_remote_copy(
            src_ref=src, dst_ref=dst,
            send_sem=g_send.at[j - 1, a, c], recv_sem=g_recv.at[j - 1, a, c],
            device_id=(peer, exp), device_id_type=MESH,
        )

    exchange = ((send_x, recv_x), (send_c, recv_c), (send_o, recv_o), (send_d, recv_d))

    def row_copy(kind, i):
        peer = lax.rem(exp + i, groups)
        src, dst = exchange[kind]
        return pltpu.make_async_remote_copy(
            src_ref=src.at[peer], dst_ref=dst.at[exp],
            send_sem=a_send.at[kind, i - 1], recv_sem=a_recv.at[kind, i - 1],
            device_id=(rep, peer), device_id_type=MESH,
        )

    def start_rows(kind):
        def step(k, carry):
            i = groups // 2 + (1 - 2 * lax.rem(k, 2)) * ((k + 1) // 2)
            row_copy(kind, i).start()
            return carry

        lax.fori_loop(0, groups - 1, step, 0)
        src, dst = exchange[kind]
        pltpu.make_async_copy(src.at[exp], dst.at[exp], local_sem.at[3 + kind]).start()

    def finish_rows(kind):
        def step(i, carry):
            row_copy(kind, i).wait_recv()
            return carry

        lax.fori_loop(1, groups, step, 0)
        src, dst = exchange[kind]
        pltpu.make_async_copy(src.at[exp], dst.at[exp], local_sem.at[3 + kind]).wait()

    loads[2].wait()
    send_x[...] = mm(select, tok[...], NN).reshape(groups, cap, features).astype(BF16)
    start_rows(0)
    row_weight = jnp.sum(
        sel0 * cw_val[0:1, :] + sel1 * cw_val[1:2, :], axis=1, keepdims=True
    )
    loads[3].wait()
    send_c[...] = (
        (mm(select, cot[...], NN) * row_weight).reshape(groups, cap, features).astype(BF16)
    )
    start_rows(1)

    table = jnp.where(
        expert == 0, dest[0],
        jnp.where(expert == 1, dest[1],
                  jnp.where(expert == 2, cw_val[0:1, :],
                            jnp.where(expert == 3, cw_val[1:2, :], 0.0))),
    )
    flipped = jnp.transpose(table)
    across = lax.broadcasted_iota(jnp.int32, (tokens, rows), 1).astype(F32)
    at0 = (across == flipped[:, 0:1]).astype(F32)
    at1 = (across == flipped[:, 1:2]).astype(F32)
    pick[...] = (at0 + at1).astype(BF16)
    weighted = at0 * flipped[:, 2:3] + at1 * flipped[:, 3:4]
    high = weighted.astype(BF16)
    pick_hi[...] = high
    pick_lo[...] = (weighted - high.astype(F32)).astype(BF16)

    for copy in own_copies:
        copy.wait()
    finish_rows(0)
    flip_x[...] = jnp.transpose(rows_2d(recv_x[...]))

    def forward(c, carry):
        x = rows_2d(recv_x[...])
        for j in range(1, reps):
            weight_copy(0, c, j).wait_recv()
        gate = mm(x, full_g[:, cols(c)], NN)
        for j in range(1, reps):
            weight_copy(1, c, j).wait_recv()
        up = mm(x, full_u[:, cols(c)], NN)
        sigma = jax.nn.sigmoid(gate)
        swish = gate * sigma
        hid[:, cols(c)] = (swish * up).astype(BF16)
        slope_u[:, cols(c)] = swish
        slope_g[:, cols(c)] = up * sigma * (1.0 + gate * (1.0 - sigma))
        return carry

    def backward(c):
        grad_h = mm(rows_2d(recv_c[...]), full_d[cols(c), :], NT)
        d_gate[:, cols(c)] = (grad_h * slope_g[:, cols(c)]).astype(BF16)
        d_up[:, cols(c)] = (grad_h * slope_u[:, cols(c)]).astype(BF16)

    def gradients(c, carry):
        part_g[:, cols(c)] = mm(flip_x[...], d_gate[:, cols(c)], NN).astype(BF16)
        for j in range(1, reps):
            grad_copy(0, c, j).start()
        part_u[:, cols(c)] = mm(flip_x[...], d_up[:, cols(c)], NN).astype(BF16)
        for j in range(1, reps):
            grad_copy(1, c, j).start()
        part_d[cols(c), :] = mm(hid[:, cols(c)], rows_2d(recv_c[...]), TN).astype(BF16)
        for j in range(1, reps):
            grad_copy(2, c, j).start()
        return carry

    lax.fori_loop(0, chunks, forward, 0)
    finish_rows(1)
    for c in range(chunks):
        for j in range(1, reps):
            weight_copy(2, c, j).wait_recv()
        if c == last:
            send_o[...] = (
                mm(hid[...], full_d[...], NN).reshape(groups, cap, features).astype(BF16)
            )
            start_rows(2)
        backward(c)
        if c == 0 and last > 0:
            gradients(0, 0)
    send_d[...] = (
        (mm(d_gate[...], full_g[...], NT) + mm(d_up[...], full_u[...], NT))
        .reshape(groups, cap, features)
        .astype(BF16)
    )
    start_rows(3)
    lax.fori_loop(min(1, last), chunks, gradients, 0)

    writes = []

    def write(src, dst):
        copy = pltpu.make_async_copy(src, dst, out_sem.at[len(writes)])
        copy.start()
        writes.append(copy)

    def average(c):
        for a in range(3):
            for j in range(1, reps):
                grad_copy(a, c, j).wait_recv()
            own, red, mean, out = (
                (part_g, red_g, gate_grad, out_gate),
                (part_u, red_u, up_grad, out_up),
                (part_d, red_d, down_grad, out_down),
            )[a]
            here, there = ((slice(None), cols(c)), (mine, cols(c)))
            if a == 2:
                here, there = ((cols(c), slice(None)), (cols(c), mine))
            total = own[there].astype(F32)
            for j in range(1, reps):
                total = total + red[(j - 1,) + here].astype(F32)
            mean[here] = (total / reps).astype(BF16)
            write(mean.at[here], out.at[here])

    def grads_sent(c):
        for a in range(3):
            for j in range(1, reps):
                grad_copy(a, c, j).wait_send()

    def rows_sent(kind):
        def step(i, carry):
            row_copy(kind, i).wait_send()
            return carry

        lax.fori_loop(1, groups, step, 0)

    rows_sent(0)
    rows_sent(1)
    for c in range(chunks):
        for a in range(3):
            for j in range(1, reps):
                weight_copy(a, c, j).wait_send()
    finish_rows(2)
    back = rows_2d(recv_o[...])
    mixed[...] = (mm(pick_hi[...], back, NN) + mm(pick_lo[...], back, NN)).astype(BF16)
    write(mixed, out_mixed)
    for c in range(last):
        average(c)
        grads_sent(c)
    rows_sent(2)
    finish_rows(3)
    token_grad[...] = mm(pick[...], rows_2d(recv_d[...]), NN).astype(BF16)
    write(token_grad, out_tokens)
    rows_sent(3)
    average(last)

    grads_sent(last)
    for copy in writes:
        copy.wait()


def hand_out(count, pieces, *refs):
    sources, targets, stages = refs[:count], refs[count : 2 * count], refs[2 * count : 3 * count]
    sems = refs[-1]
    loads, stores = [], []
    for k in reversed(range(count)):
        size = sources[k].shape[0] // pieces
        for p in range(pieces):
            part, at = pl.ds(p * size, size), k * pieces + p
            loads.append(
                pltpu.make_async_copy(sources[k].at[part], stages[k].at[part], sems.at[0, at])
            )
            stores.append(
                pltpu.make_async_copy(stages[k].at[part], targets[k].at[part], sems.at[1, at])
            )
    for load in loads:
        load.start()
    for load, store in zip(loads, stores):
        load.wait()
        store.start()
    for store in stores:
        store.wait()


def per_device(reps, groups, tokens, cotangent, expert_ids, combine_weight, gate_w, up_w, down_w):
    tok_rows, features = tokens.shape
    top = expert_ids.shape[1]
    share, hidden = gate_w.shape[1:]
    cap = 2 * tok_rows * top // groups
    rows = groups * cap
    width = 256
    chunks = hidden // width
    pieces = 4
    anywhere = pl.BlockSpec(memory_space=pl.ANY)
    block = pltpu.VMEM((groups, cap, features), BF16)
    act = pltpu.VMEM((rows, hidden), BF16)
    dma = pltpu.SemaphoreType.DMA
    others = reps - 1
    shapes = (
        jax.ShapeDtypeStruct((tok_rows, features), BF16),
        jax.ShapeDtypeStruct((tok_rows, features), BF16),
        jax.ShapeDtypeStruct((share, hidden), BF16),
        jax.ShapeDtypeStruct((share, hidden), BF16),
        jax.ShapeDtypeStruct((hidden, share), BF16),
    )
    outs = pl.pallas_call(
        functools.partial(kernel, reps, groups, cap, width),
        out_shape=shapes,
        in_specs=[anywhere] * 7,
        out_specs=(anywhere,) * 5,
        scratch_shapes=[block] * 8
        + [
            pltpu.VMEM((features, hidden), BF16),
            pltpu.VMEM((features, hidden), BF16),
            pltpu.VMEM((hidden, features), BF16),
        ]
        + [act] * 3
        + [
            pltpu.VMEM((features, hidden), BF16),
            pltpu.VMEM((features, hidden), BF16),
            pltpu.VMEM((hidden, features), BF16),
            pltpu.VMEM((others, share, hidden), BF16),
            pltpu.VMEM((others, share, hidden), BF16),
            pltpu.VMEM((others, hidden, share), BF16),
        ]
        + [pltpu.VMEM((tok_rows, rows), BF16)] * 3
        + [pltpu.VMEM((features, rows), BF16)]
        + [pltpu.VMEM((rows, hidden), F32)] * 2
        + [pltpu.VMEM(shape.shape, BF16) for shape in shapes]
        + [
            pltpu.VMEM((tok_rows, features), BF16),
            pltpu.VMEM((tok_rows, features), BF16),
            pltpu.VMEM((top, tok_rows), jnp.int32),
            pltpu.VMEM((top, tok_rows), F32),
        ]
        + [
            dma((4, groups - 1)),
            dma((4, groups - 1)),
            dma((others, 3, chunks)),
            dma((others, 3, chunks)),
            dma((others, 3, chunks)),
            dma((others, 3, chunks)),
            dma((11,)),
            dma((2 + 3 * chunks,)),
        ],
        compiler_params=pltpu.CompilerParams(
            collective_id=0, has_side_effects=True, vmem_limit_bytes=56 * 1024 * 1024
        ),
        cost_estimate=pl.CostEstimate(
            flops=18 * rows * features * hidden,
            bytes_accessed=16 * share * hidden,
            transcendentals=rows * hidden,
        ),
    )(tokens, cotangent, expert_ids.T, combine_weight.T, gate_w[0], up_w[0], down_w[0])
    mixed, token_grad, gate_grad, up_grad, down_grad = pl.pallas_call(
        functools.partial(hand_out, len(shapes), pieces),
        out_shape=shapes,
        in_specs=[anywhere] * len(shapes),
        out_specs=(anywhere,) * len(shapes),
        scratch_shapes=[pltpu.VMEM(shape.shape, BF16) for shape in shapes] + [dma((2, len(shapes) * pieces))],
        compiler_params=pltpu.CompilerParams(vmem_limit_bytes=60 * 1024 * 1024),
    )(*outs)
    return mixed, token_grad, gate_grad[None], up_grad[None], down_grad[None]


def solution(mesh):
    placed = (
        P(("rep", "exp"), None),
        P(("rep", "exp"), None),
        P(("rep", "exp"), None),
        P(("rep", "exp"), None),
        P("exp", "rep", None),
        P("exp", "rep", None),
        P("exp", None, "rep"),
    )
    return jax.shard_map(
        functools.partial(per_device, mesh.shape["rep"], mesh.shape["exp"]),
        mesh=mesh,
        in_specs=placed,
        out_specs=(
            P(("rep", "exp"), None),
            P(("rep", "exp"), None),
            P("exp", "rep", None),
            P("exp", "rep", None),
            P("exp", None, "rep"),
        ),
        check_vma=False,
    )
```
